32 devices in a mesh: dp: 4 (over y, x), seq: 8 (over z, core).
Axes of the slice: x: 2, y: 2, z: 4, core: 2. Of those that a mesh axis runs over, the one named last changes fastest.
Arguments:
- query_tok: bfloat16 [4, 1024, 2560], P('dp', 'seq'), may hold values from -6 to 6
- key_tok: bfloat16 [4, 1024, 2560], P('dp', 'seq'), may hold values from -6 to 6
- value_tok: bfloat16 [4, 1024, 2560], P('dp', 'seq'), may hold values from -6 to 6
- grad_out: bfloat16 [4, 1024, 5120], P('dp', 'seq'), may hold values from -6 to 6
- out_weight: bfloat16 [24, 128, 5120], P('seq', None, 'dp'), may hold values from -0.125 to 0.125
- block_mask: int32 [20, 8, 8], replicated, may hold values from 0 to 1, as said below
- head_owner: int32 [20], replicated, may hold values from 0 to 7, as said below
Outputs:
- attn_out: bfloat16 [4, 1024, 2560], P('dp', 'seq')
- query_grad: bfloat16 [4, 1024, 2560], P('dp', 'seq')
- key_grad: bfloat16 [4, 1024, 2560], P('dp', 'seq')
- value_grad: bfloat16 [4, 1024, 2560], P('dp', 'seq')
- weight_grad: float32 [24, 128, 5120], P('seq', None, 'dp')
The draws below stay inside these ranges and needn't reach their ends.
Inputs may be any that keep to these rules, and one draw needn't show every extreme that they name: `block_mask`: every diagonal tile is 1; each head has its own share of other tiles. `head_owner`: each value is an index of seq; no index holds more than 3 heads, and some index holds exactly 3.
All inputs are finite; a program needn't handle non-finite values.
Results may differ from the reference program's by a relative error of at most 0.017.
Values may be sent and summed in bfloat16 or wider, within the bound.
A program may use at most 128 MiB of HBM per device.

```python
import jax
import jax.numpy as jnp
from jax import lax

D = 5120
HEADS = 20
HDIM = 128
HD = 2560
BLOCK = 128
TOKENS = 1024
CLIPS = 4
MOST = 3
SLOTS = 24
NB = 8


def paired_draw(key):
    shape = (CLIPS, TOKENS, HD)
    queries = jnp.clip(jax.random.normal(jax.random.fold_in(key, 11), shape), -6.0, 6.0)
    keys_all = jnp.clip(jax.random.normal(jax.random.fold_in(key, 12), shape), -6.0, 6.0)
    return (queries, keys_all)


def draw_query_tok(key, part):
    return paired_draw(key)[0].astype(jnp.bfloat16)


def draw_key_tok(key, part):
    return paired_draw(key)[1].astype(jnp.bfloat16)


def draw_block_mask(key, part):
    density = jax.random.randint(jax.random.fold_in(key, 31), (HEADS, 1, 1), 100, 251)
    levels = jax.random.randint(jax.random.fold_in(key, 32), (HEADS, NB, NB), 0, 1000)
    diagonal = jnp.arange(NB)[:, None] == jnp.arange(NB)[None, :]
    kept = jnp.logical_or(levels < density, diagonal[None, :, :])
    return jnp.where(kept, 1, 0).astype(jnp.int32)


def draw_head_owner(key, part):
    order = jax.random.permutation(jax.random.fold_in(key, 41), SLOTS)
    return (order[:HEADS] // MOST).astype(jnp.int32)


def block_levels(own_key, shape, shards, smallest, top_value):
    level, own = 1.0, jax.random.fold_in(own_key, 6)
    for dim, parts in shards:
        steps = jnp.exp(jax.random.uniform(jax.random.fold_in(own, dim), (parts,), jnp.float32, smallest / len(shards), top_value / len(shards)))
        level = level * jnp.repeat(steps, shape[dim] // parts).reshape([-1 if axis == dim else 1 for axis in range(len(shape))])
    return level


def centred(stream_key, extent, spread, reach, cuts=(), kind=jnp.bfloat16):
    factor_of = block_levels(stream_key, extent, cuts, -0.22, 0.18) if cuts else 1.0
    result = jax.random.normal(stream_key, extent, jnp.float32) * spread * factor_of
    return jnp.minimum(jnp.maximum(result, -reach), reach).astype(kind)


def setup_inputs(seed: int = 0) -> dict:
    key_of = jax.random.split(jax.random.key(seed), 8)
    query_tok = draw_query_tok(jax.random.fold_in(key_of[7], 71), 0)
    key_tok = draw_key_tok(jax.random.fold_in(key_of[7], 71), 0)
    value_tok = centred(key_of[2], (CLIPS, TOKENS, HD), 1.0, 6.0, ((0, 4), (1, 8)))
    grad_out = centred(key_of[3], (CLIPS, TOKENS, D), 1.0, 6.0, ((0, 4), (1, 8)))
    out_weight = centred(key_of[4], (SLOTS, HDIM, D), HD ** -0.5, 0.125, ((0, 8), (2, 4)))
    block_mask = draw_block_mask(jax.random.fold_in(key_of[7], 71), 0)
    head_owner = draw_head_owner(jax.random.fold_in(key_of[7], 71), 0)
    return {"query_tok": query_tok, "key_tok": key_tok, "value_tok": value_tok, "grad_out": grad_out, "out_weight": out_weight, "block_mask": block_mask, "head_owner": head_owner}


def slot_index(head_owner):
    same_owner = head_owner[:, None] == head_owner[None, :]
    earlier = jnp.arange(HEADS)[None, :] < jnp.arange(HEADS)[:, None]
    owner_rank = jnp.sum(jnp.logical_and(same_owner, earlier), axis=1).astype(jnp.int32)
    return (head_owner * MOST + owner_rank).astype(jnp.int32)


def one_head(queries, keys_all, values_all, cotangent, weight_rows, tiles):
    score_scale = HDIM ** -0.5
    scores = jnp.dot(queries, keys_all.T, preferred_element_type=jnp.float32) * score_scale
    allowed = jnp.repeat(jnp.repeat(tiles, BLOCK, axis=0), BLOCK, axis=1) > 0
    scores = jnp.where(allowed, scores, -jnp.inf)
    row_max = jnp.max(scores, axis=1, keepdims=True)
    expd = jnp.exp(scores - row_max)
    attn_prob = expd / jnp.sum(expd, axis=1, keepdims=True)
    prob_low = attn_prob.astype(jnp.bfloat16)
    attn_out = jnp.dot(prob_low, values_all, preferred_element_type=jnp.float32).astype(jnp.bfloat16)
    grad_attn = jnp.dot(cotangent, weight_rows.T, preferred_element_type=jnp.float32).astype(jnp.bfloat16)
    weight_part = jnp.dot(attn_out.T, cotangent, preferred_element_type=jnp.float32)
    value_grad = jnp.dot(prob_low.T, grad_attn, preferred_element_type=jnp.float32).astype(jnp.bfloat16)
    prob_grad = jnp.dot(grad_attn, values_all.T, preferred_element_type=jnp.float32)
    row_delta = jnp.sum(grad_attn.astype(jnp.float32) * attn_out.astype(jnp.float32), axis=1, keepdims=True)
    score_grad = (attn_prob * (prob_grad - row_delta) * score_scale).astype(jnp.bfloat16)
    query_grad = jnp.dot(score_grad, keys_all, preferred_element_type=jnp.float32).astype(jnp.bfloat16)
    key_grad = jnp.dot(score_grad.T, queries, preferred_element_type=jnp.float32).astype(jnp.bfloat16)
    return attn_out, query_grad, key_grad, value_grad, weight_part


def reference(query_tok, key_tok, value_tok, grad_out, out_weight, block_mask, head_owner):
    slots = slot_index(head_owner)
    head_rows = jnp.take(out_weight, slots, axis=0)

    def by_head(tensor):
        return jnp.transpose(tensor.reshape(CLIPS, TOKENS, HEADS, HDIM), (2, 0, 1, 3))

    q_heads = by_head(query_tok)
    k_heads = by_head(key_tok)
    v_heads = by_head(value_tok)

    def head_work(packed):
        queries, keys_all, values_all, weight_rows, tiles = packed

        def clip_work(inner):
            return one_head(inner[0], inner[1], inner[2], inner[3], weight_rows, tiles)

        outs_all = lax.map(clip_work, (queries, keys_all, values_all, grad_out))
        weight_sum = jnp.sum(outs_all[4], axis=0) * ((CLIPS * TOKENS) ** -0.5)
        return outs_all[0], outs_all[1], outs_all[2], outs_all[3], weight_sum

    results = lax.map(head_work, (q_heads, k_heads, v_heads, head_rows, block_mask))

    def by_token(tensor):
        return jnp.transpose(tensor, (1, 2, 0, 3)).reshape(CLIPS, TOKENS, HD)

    weight_grad = jnp.zeros((SLOTS, HDIM, D), jnp.float32).at[slots].set(results[4])
    return by_token(results[0]), by_token(results[1]), by_token(results[2]), by_token(results[3]), weight_grad
```

```python
import functools

import jax
import jax.numpy as jnp
from jax import lax
from jax.experimental import pallas as pl
from jax.experimental.pallas import tpu as pltpu
from jax.sharding import PartitionSpec as P

F32 = jnp.float32
BF16 = jnp.bfloat16
NT = (((1,), (1,)), ((), ()))
TN = (((0,), (0,)), ((), ()))
NN = (((1,), (0,)), ((), ()))


def dot(a, b, dims):
    return lax.dot_general(a, b, dims, preferred_element_type=F32)


def slot_numbers(head_owner, most):
    count = head_owner.shape[0]
    same = head_owner[:, None] == head_owner[None, :]
    earlier = jnp.arange(count)[None, :] < jnp.arange(count)[:, None]
    rank = jnp.sum(jnp.logical_and(same, earlier), axis=1).astype(jnp.int32)
    return head_owner * most + rank


def forward_kernel(scale, bias_ref, qkv_ref, out_ref, lse_ref):
    blocks, rows, dim = qkv_ref.shape[0], qkv_ref.shape[3], qkv_ref.shape[4]
    keys = qkv_ref[:, 0, 1].reshape(blocks * rows, dim)
    values = qkv_ref[:, 0, 2].reshape(blocks * rows, dim)
    slot = pl.program_id(0)

    @pl.loop(0, blocks)
    def _(i):
        q = qkv_ref[i, 0, 0]
        scores = dot(keys, q, NT) * scale
        parts = [
            scores[j * rows : (j + 1) * rows] + bias_ref[slot, i, j] for j in range(blocks)
        ]
        top = jnp.max(functools.reduce(jnp.maximum, parts), axis=0, keepdims=True)
        parts = [jnp.exp(part - top) for part in parts]
        total = jnp.sum(functools.reduce(jnp.add, parts), axis=0, keepdims=True)
        inverse = 1.0 / total
        low = jnp.concatenate([(part * inverse).astype(BF16) for part in parts], axis=0)
        out_ref[i, 0] = dot(low, values, TN).astype(BF16)
        lse_ref[0, pl.ds(i, 1), :] = top + jnp.log(total)


def backward_kernel(scale, bias_ref, qkv_ref, out_in_ref, lse_ref, grad_ref, out_ref, dk_ref, dv_ref):
    blocks, rows, dim = qkv_ref.shape[0], qkv_ref.shape[3], qkv_ref.shape[4]
    keys = qkv_ref[:, 0, 1].reshape(blocks * rows, dim)
    values = qkv_ref[:, 0, 2].reshape(blocks * rows, dim)
    slot = pl.program_id(0)
    dk_ref[...] = jnp.zeros_like(dk_ref)
    dv_ref[...] = jnp.zeros_like(dv_ref)

    @pl.loop(0, blocks)
    def _(i):
        q = qkv_ref[i, 0, 0]
        g = grad_ref[0, pl.ds(pl.multiple_of(i * rows, rows), rows), :]
        product = g.astype(F32) * out_in_ref[i, 0].astype(F32)
        delta = jnp.sum(product.T, axis=0, keepdims=True)
        lse = lse_ref[0, pl.ds(i, 1), :]
        scores = dot(keys, q, NT) * scale
        prob_grad = dot(values, g, NT)
        lows, grads = [], []
        for j in range(blocks):
            part = slice(j * rows, (j + 1) * rows)
            prob = jnp.exp(scores[part] + (bias_ref[slot, i, j] - lse))
            lows.append(prob.astype(BF16))
            grads.append((prob * (prob_grad[part] - delta) * scale).astype(BF16))
        low = jnp.concatenate(lows, axis=0)
        score_grad = jnp.concatenate(grads, axis=0)
        dv_ref[...] += dot(low, g, NN)
        dk_ref[...] += dot(score_grad, q, NN)
        out_ref[i, 0, 0] = dot(score_grad, keys, TN).astype(BF16)

    out_ref[:, 0, 1] = dk_ref[...].astype(BF16).reshape(blocks, rows, dim)
    out_ref[:, 0, 2] = dv_ref[...].astype(BF16).reshape(blocks, rows, dim)


def tokens_kernel(heads, slot_ref, *refs):
    count = len(refs) // 2
    dim = refs[0].shape[-1]
    for source, target in zip(refs[:count], refs[count:]):
        for h in range(heads):
            target[0, :, h * dim : (h + 1) * dim] = source[slot_ref[h]]


SMEM = pl.BlockSpec(memory_space=pltpu.SMEM)
VMEM = pl.BlockSpec(memory_space=pltpu.VMEM)
PARAMS = pltpu.CompilerParams(vmem_limit_bytes=48 * 1024 * 1024)


def on_device(query_tok, key_tok, value_tok, grad_out, out_weight, block_mask, head_owner):
    seq = lax.axis_size("seq")
    dps = lax.axis_size("dp")
    most, dim, part_width = out_weight.shape
    rows = query_tok.shape[1]
    heads = block_mask.shape[0]
    tiles = block_mask.shape[1]
    length = seq * rows
    width = grad_out.shape[2]
    scale = dim ** (-0.5)
    grad_scale = (dps * length) ** (-0.5)
    slots = slot_numbers(head_owner, most)
    table = slots[:, None] == jnp.arange(seq * most, dtype=jnp.int32)[None, :]
    select = table.astype(BF16)
    mine = lax.dynamic_slice_in_dim(table, lax.axis_index("seq") * most, most, 1)
    used = jnp.any(mine, axis=0)
    kept = jnp.any(
        jnp.logical_and(mine[:, :, None, None], block_mask[:, None] > 0), axis=0
    ) | jnp.logical_not(used)[:, None, None]
    bias = jnp.where(kept, 0.0, -jnp.inf).astype(F32)

    def to_slots(tensor):
        split = tensor[0].reshape(rows, heads, dim)
        spread = jnp.einsum("thd,hj->jtd", split, select, preferred_element_type=F32)
        return spread.astype(BF16).reshape(seq, most, 1, rows, dim)

    dy = lax.all_gather(grad_out, "seq", axis=1, tiled=True)[0]
    sent = jnp.concatenate([to_slots(t) for t in (query_tok, key_tok, value_tok)], axis=2)
    qkv = lax.all_to_all(sent, "seq", split_axis=0, concat_axis=0, tiled=True)
    weight_full = lax.all_gather(out_weight, "dp", axis=2, tiled=True)

    qkv_spec = pl.BlockSpec((seq, 1, 3, rows, dim), lambda s: (0, s, 0, 0, 0))
    out_spec = pl.BlockSpec((seq, 1, rows, dim), lambda s: (0, s, 0, 0))
    lse_spec = pl.BlockSpec((1, tiles, rows), lambda s: (s, 0, 0))
    slot_out, lse = pl.pallas_call(
        functools.partial(forward_kernel, scale),
        grid=(most,),
        out_shape=(
            jax.ShapeDtypeStruct((seq, most, rows, dim), BF16),
            jax.ShapeDtypeStruct((most, tiles, rows), F32),
        ),
        in_specs=[SMEM, qkv_spec],
        out_specs=(out_spec, lse_spec),
        compiler_params=PARAMS,
        name="attention_forward",
    )(bias, qkv)
    out_back = lax.all_to_all(slot_out, "seq", split_axis=0, concat_axis=0, tiled=True)

    grad_attn = jnp.einsum("td,shd->sth", dy, weight_full, preferred_element_type=F32).astype(BF16)
    grads = pl.pallas_call(
        functools.partial(backward_kernel, scale),
        grid=(most,),
        out_shape=jax.ShapeDtypeStruct((seq, most, 3, rows, dim), BF16),
        in_specs=[
            SMEM,
            qkv_spec,
            out_spec,
            lse_spec,
            pl.BlockSpec((1, length, dim), lambda s: (s, 0, 0)),
        ],
        out_specs=qkv_spec,
        scratch_shapes=[pltpu.VMEM((length, dim), F32), pltpu.VMEM((length, dim), F32)],
        compiler_params=PARAMS,
        name="attention_backward",
    )(bias, qkv, slot_out, lse, grad_attn)
    grads_back = lax.all_to_all(grads, "seq", split_axis=0, concat_axis=0, tiled=True)

    weight_total = jnp.einsum(
        "asth,atd->shd", slot_out.reshape(seq, most, rows, dim), dy.reshape(seq, rows, width),
        preferred_element_type=F32,
    )
    weight_low = (weight_total * grad_scale).astype(BF16).reshape(most, dim, dps, part_width)
    weight_parts = lax.all_to_all(
        weight_low.transpose(2, 0, 1, 3), "dp", split_axis=0, concat_axis=0, tiled=True
    )
    weight_grad = jnp.sum(weight_parts.astype(F32), axis=0)
    weight_grad = jnp.where(used[:, None, None], weight_grad, 0.0)

    token_shape = jax.ShapeDtypeStruct((1, rows, heads * dim), BF16)
    flat = (seq * most, rows, dim)
    attn_out, query_grad, key_grad, value_grad = pl.pallas_call(
        functools.partial(tokens_kernel, heads),
        out_shape=(token_shape,) * 4,
        in_specs=[SMEM] + [VMEM] * 4,
        out_specs=(VMEM,) * 4,
        compiler_params=PARAMS,
        name="heads_to_tokens",
    )(
        slots,
        out_back.reshape(flat),
        grads_back[:, :, 0].reshape(flat),
        grads_back[:, :, 1].reshape(flat),
        grads_back[:, :, 2].reshape(flat),
    )
    return (attn_out, query_grad, key_grad, value_grad, weight_grad)


def solution(mesh):
    placed = (
        P("dp", "seq", None),
        P("dp", "seq", None),
        P("dp", "seq", None),
        P("dp", "seq", None),
        P("seq", None, "dp"),
        P(),
        P(),
    )
    return jax.shard_map(
        on_device,
        mesh=mesh,
        in_specs=placed,
        out_specs=(
            P("dp", "seq", None),
            P("dp", "seq", None),
            P("dp", "seq", None),
            P("dp", "seq", None),
            P("seq", None, "dp"),
        ),
        check_vma=False,
    )
```

```python
import functools

import jax
import jax.numpy as jnp
from jax import lax
from jax.experimental import pallas as pl
from jax.experimental.pallas import tpu as pltpu
from jax.sharding import PartitionSpec as P

F32 = jnp.float32
BF16 = jnp.bfloat16
NT = (((1,), (1,)), ((), ()))
TN = (((0,), (0,)), ((), ()))
NN = (((1,), (0,)), ((), ()))


def dot(a, b, dims):
    return lax.dot_general(a, b, dims, preferred_element_type=F32)


def slot_numbers(head_owner, most):
    count = head_owner.shape[0]
    same = head_owner[:, None] == head_owner[None, :]
    earlier = jnp.arange(count)[None, :] < jnp.arange(count)[:, None]
    rank = jnp.sum(jnp.logical_and(same, earlier), axis=1).astype(jnp.int32)
    return head_owner * most + rank


def gather_kernel(
    scale, bias_ref, sent_ref, dy_ref, weight_ref, qkv_ref, dy_all, out_ref, lse_ref, grad_ref,
    weight_all, dy_block, own_sem, qkv_send, qkv_recv, weight_send, weight_recv,
    right_send, left_send, chain_recv, pair_send, pair_recv, load_sem,
):
    seq, most, _, rows, dim = qkv_ref.shape
    dps = weight_all.shape[0]
    chips = seq // 2
    me, dp = lax.axis_index("seq"), lax.axis_index("dp")
    chip, core = me // 2, lax.rem(me, 2)
    pair = me + 1 - 2 * core

    def remote(source, target, send_sem, recv_sem, where):
        return pltpu.make_async_remote_copy(
            src_ref=source, dst_ref=target, send_sem=send_sem, recv_sem=recv_sem,
            device_id=where, device_id_type=pl.DeviceIdType.MESH,
        )

    barrier = pltpu.get_barrier_semaphore()
    for k in range(1, seq):
        pl.semaphore_signal(
            barrier, inc=1, device_id=(dp, lax.rem(me + k, seq)), device_id_type=pl.DeviceIdType.MESH
        )
    for k in range(1, dps):
        pl.semaphore_signal(
            barrier, inc=1, device_id=(lax.rem(dp + k, dps), me), device_id_type=pl.DeviceIdType.MESH
        )
    pl.semaphore_wait(barrier, seq - 1 + dps - 1)

    own = [
        pltpu.make_async_copy(sent_ref.at[me], qkv_ref.at[me], own_sem.at[0]),
        pltpu.make_async_copy(dy_ref.at[0], dy_all.at[me], own_sem.at[1]),
        pltpu.make_async_copy(weight_ref, weight_all.at[dp], own_sem.at[2]),
    ]
    qkv_copies = []
    for k in range(1, seq):
        to = lax.rem(me + k, seq)
        qkv_copies.append(
            remote(sent_ref.at[to], qkv_ref.at[me], qkv_send.at[k], qkv_recv.at[k], (dp, to))
        )
    weight_copies = [
        remote(weight_ref, weight_all.at[dp], weight_send.at[k], weight_recv.at[k],
               (lax.rem(dp + k, dps), me))
        for k in range(1, dps)
    ]

    def right_copy(source, origin):
        return remote(source, dy_all.at[2 * origin + core], right_send.at[origin],
                      chain_recv.at[origin], (dp, me + 2))

    def left_copy(source, origin):
        return remote(source, dy_all.at[2 * origin + core], left_send.at[origin],
                      chain_recv.at[origin], (dp, me - 2))

    def pair_copy(source, origin):
        return remote(source, dy_all.at[2 * origin + core], pair_send.at[origin],
                      pair_recv.at[origin], (dp, pair))

    for copy in qkv_copies + weight_copies + own:
        copy.start()

    @pl.when(chip + 1 < chips)
    def _():
        right_copy(dy_ref.at[0], chip).start()

    @pl.when(chip > 0)
    def _():
        left_copy(dy_ref.at[0], chip).start()

    pair_copy(dy_ref.at[0], chip).start()

    def pass_on(step):
        @pl.when(chip - 1 - step >= 0)
        def _():
            origin = chip - 1 - step
            block = dy_all.at[2 * origin + core]
            right_copy(block, origin).wait_recv()

            @pl.when(chip + 1 < chips)
            def _():
                right_copy(block, origin).start()

            pair_copy(block, origin).start()

        @pl.when(chip + 1 + step < chips)
        def _():
            origin = chip + 1 + step
            block = dy_all.at[2 * origin + core]
            left_copy(block, origin).wait_recv()

            @pl.when(chip > 0)
            def _():
                left_copy(block, origin).start()

            pair_copy(block, origin).start()

    for copy in qkv_copies:
        copy.wait_recv()
    own[0].wait()

    def forward(slot):
        keys = qkv_ref[:, slot, 1].reshape(seq * rows, dim)
        values = qkv_ref[:, slot, 2].reshape(seq * rows, dim)

        @pl.loop(0, seq)
        def _(i):
            q = qkv_ref[i, slot, 0]
            scores = dot(keys, q, NT) * scale
            parts = [
                scores[j * rows : (j + 1) * rows] + bias_ref[slot, i, j] for j in range(seq)
            ]
            top = jnp.max(functools.reduce(jnp.maximum, parts), axis=0, keepdims=True)
            parts = [jnp.exp(part - top) for part in parts]
            total = jnp.sum(functools.reduce(jnp.add, parts), axis=0, keepdims=True)
            inverse = 1.0 / total
            low = jnp.concatenate([(part * inverse).astype(BF16) for part in parts], axis=0)
            out_ref[i, slot] = dot(low, values, TN).astype(BF16)
            lse_ref[slot, pl.ds(i, 1), :] = top + jnp.log(total)

    def project(block):
        load = pltpu.make_async_copy(dy_all.at[block], dy_block, load_sem)
        load.start()
        load.wait()
        part_width = weight_all.shape[3]
        total = None
        for d in range(dps):
            term = dot(
                dy_block[:, d * part_width : (d + 1) * part_width],
                weight_all[d].reshape(most * dim, part_width), NT,
            )
            total = term if total is None else total + term
        for s in range(most):
            grad_ref[s, pl.ds(pl.multiple_of(block * rows, rows), rows), :] = total[
                :, s * dim : (s + 1) * dim
            ].astype(BF16)

    def project_ring(k):
        for origin, wanted in (
            (chip - k, chip - k >= 0),
            (chip + k, jnp.logical_and(k > 0, chip + k < chips)),
        ):
            @pl.when(wanted)
            def _(origin=origin):
                project(2 * origin + core)
                pair_copy(dy_all.at[2 * origin + core], origin).wait_recv()
                project(2 * origin + 1 - core)

    for step in range(max(chips - 1, most)):
        if step < most:
            forward(step)
        if step < chips - 1:
            pass_on(step)
        if step == 0:
            own[1].wait()
            own[2].wait()
            for copy in weight_copies:
                copy.wait_recv()
        if step < chips - 1:
            project_ring(step)
    project_ring(chips - 1)

    for copy in qkv_copies + weight_copies:
        copy.wait_send()
    for origin in range(chips):
        block = dy_all.at[2 * origin + core]
        pair_copy(block, origin).wait_send()

        @pl.when(jnp.logical_and(chip + 1 < chips, origin <= chip))
        def _():
            right_copy(block, origin).wait_send()

        @pl.when(jnp.logical_and(chip > 0, origin >= chip))
        def _():
            left_copy(block, origin).wait_send()


def backward_kernel(scale, bias_ref, qkv_ref, out_in_ref, lse_ref, grad_ref, out_ref, dk_ref, dv_ref):
    blocks, rows, dim = qkv_ref.shape[0], qkv_ref.shape[3], qkv_ref.shape[4]
    keys = qkv_ref[:, 0, 1].reshape(blocks * rows, dim)
    values = qkv_ref[:, 0, 2].reshape(blocks * rows, dim)
    slot = pl.program_id(0)
    dk_ref[...] = jnp.zeros_like(dk_ref)
    dv_ref[...] = jnp.zeros_like(dv_ref)

    @pl.loop(0, blocks)
    def _(i):
        q = qkv_ref[i, 0, 0]
        g = grad_ref[0, pl.ds(pl.multiple_of(i * rows, rows), rows), :]
        product = g.astype(F32) * out_in_ref[i, 0].astype(F32)
        delta = jnp.sum(product.T, axis=0, keepdims=True)
        lse = lse_ref[0, pl.ds(i, 1), :]
        scores = dot(keys, q, NT) * scale
        prob_grad = dot(values, g, NT)
        lows, grads = [], []
        for j in range(blocks):
            part = slice(j * rows, (j + 1) * rows)
            prob = jnp.exp(scores[part] + (bias_ref[slot, i, j] - lse))
            lows.append(prob.astype(BF16))
            grads.append((prob * (prob_grad[part] - delta) * scale).astype(BF16))
        low = jnp.concatenate(lows, axis=0)
        score_grad = jnp.concatenate(grads, axis=0)
        dv_ref[...] += dot(low, g, NN)
        dk_ref[...] += dot(score_grad, q, NN)
        out_ref[i, 0, 0] = dot(score_grad, keys, TN).astype(BF16)

    out_ref[:, 0, 1] = dk_ref[...].astype(BF16).reshape(blocks, rows, dim)
    out_ref[:, 0, 2] = dv_ref[...].astype(BF16).reshape(blocks, rows, dim)


def tokens_kernel(heads, slot_ref, *refs):
    count = len(refs) // 2
    dim = refs[0].shape[-1]
    for source, target in zip(refs[:count], refs[count:]):
        for h in range(heads):
            target[0, :, h * dim : (h + 1) * dim] = source[slot_ref[h]]


SMEM = pl.BlockSpec(memory_space=pltpu.SMEM)
VMEM = pl.BlockSpec(memory_space=pltpu.VMEM)
ANY = pl.BlockSpec(memory_space=pl.ANY)
PARAMS = pltpu.CompilerParams(vmem_limit_bytes=48 * 1024 * 1024)


def on_device(query_tok, key_tok, value_tok, grad_out, out_weight, block_mask, head_owner):
    seq = lax.axis_size("seq")
    dps = lax.axis_size("dp")
    most, dim, part_width = out_weight.shape
    rows = query_tok.shape[1]
    heads = block_mask.shape[0]
    tiles = block_mask.shape[1]
    length = seq * rows
    width = grad_out.shape[2]
    scale = dim ** (-0.5)
    grad_scale = (dps * length) ** (-0.5)
    slots = slot_numbers(head_owner, most)
    table = slots[:, None] == jnp.arange(seq * most, dtype=jnp.int32)[None, :]
    select = table.astype(BF16)
    mine = lax.dynamic_slice_in_dim(table, lax.axis_index("seq") * most, most, 1)
    used = jnp.any(mine, axis=0)
    kept = jnp.any(
        jnp.logical_and(mine[:, :, None, None], block_mask[:, None] > 0), axis=0
    ) | jnp.logical_not(used)[:, None, None]
    bias = jnp.where(kept, 0.0, -jnp.inf).astype(F32)

    def to_slots(tensor):
        split = tensor[0].reshape(rows, heads, dim)
        spread = jnp.einsum("thd,hj->jtd", split, select, preferred_element_type=F32)
        return spread.astype(BF16).reshape(seq, most, 1, rows, dim)

    sent = jnp.concatenate([to_slots(t) for t in (query_tok, key_tok, value_tok)], axis=2)
    qkv_spec = pl.BlockSpec((seq, 1, 3, rows, dim), lambda s: (0, s, 0, 0, 0))
    out_spec = pl.BlockSpec((seq, 1, rows, dim), lambda s: (0, s, 0, 0))
    lse_spec = pl.BlockSpec((1, tiles, rows), lambda s: (s, 0, 0))
    chips = seq // 2
    dma = pltpu.SemaphoreType.DMA
    qkv, dy, slot_out, lse, grad_attn = pl.pallas_call(
        functools.partial(gather_kernel, scale),
        out_shape=(
            jax.ShapeDtypeStruct((seq, most, 3, rows, dim), BF16),
            jax.ShapeDtypeStruct((seq, rows, width), BF16),
            jax.ShapeDtypeStruct((seq, most, rows, dim), BF16),
            jax.ShapeDtypeStruct((most, tiles, rows), F32),
            jax.ShapeDtypeStruct((most, length, dim), BF16),
        ),
        in_specs=[SMEM, ANY, ANY, ANY],
        out_specs=(VMEM, ANY, VMEM, VMEM, VMEM),
        scratch_shapes=[
            pltpu.VMEM((dps, most, dim, part_width), BF16),
            pltpu.VMEM((rows, width), BF16),
            dma((3,)), dma((seq,)), dma((seq,)), dma((dps,)), dma((dps,)),
            dma((chips,)), dma((chips,)), dma((chips,)), dma((chips,)), dma((chips,)),
            dma(()),
        ],
        compiler_params=pltpu.CompilerParams(
            vmem_limit_bytes=48 * 1024 * 1024, collective_id=0, has_side_effects=True
        ),
        name="gather_forward",
    )(bias, sent, grad_out, out_weight)
    out_back = lax.all_to_all(slot_out, "seq", split_axis=0, concat_axis=0, tiled=True)

    grads = pl.pallas_call(
        functools.partial(backward_kernel, scale),
        grid=(most,),
        out_shape=jax.ShapeDtypeStruct((seq, most, 3, rows, dim), BF16),
        in_specs=[
            SMEM,
            qkv_spec,
            out_spec,
            lse_spec,
            pl.BlockSpec((1, length, dim), lambda s: (s, 0, 0)),
        ],
        out_specs=qkv_spec,
        scratch_shapes=[pltpu.VMEM((length, dim), F32), pltpu.VMEM((length, dim), F32)],
        compiler_params=PARAMS,
        name="attention_backward",
    )(bias, qkv, slot_out, lse, grad_attn)

    dy, grads = lax.optimization_barrier((dy, grads))
    grads_back = lax.all_to_all(grads, "seq", split_axis=0, concat_axis=0, tiled=True)
    weight_total = jnp.einsum(
        "asth,atd->shd", slot_out.reshape(seq, most, rows, dim), dy,
        preferred_element_type=F32,
    )
    weight_low = (weight_total * grad_scale).astype(BF16).reshape(most, dim, dps, part_width)
    weight_parts = lax.all_to_all(
        weight_low.transpose(2, 0, 1, 3), "dp", split_axis=0, concat_axis=0, tiled=True
    )
    weight_grad = jnp.sum(weight_parts.astype(F32), axis=0)
    weight_grad = jnp.where(used[:, None, None], weight_grad, 0.0)

    token_shape = jax.ShapeDtypeStruct((1, rows, heads * dim), BF16)
    flat = (seq * most, rows, dim)
    attn_out, query_grad, key_grad, value_grad = pl.pallas_call(
        functools.partial(tokens_kernel, heads),
        out_shape=(token_shape,) * 4,
        in_specs=[SMEM] + [VMEM] * 4,
        out_specs=(VMEM,) * 4,
        compiler_params=PARAMS,
        name="heads_to_tokens",
    )(
        slots,
        out_back.reshape(flat),
        grads_back[:, :, 0].reshape(flat),
        grads_back[:, :, 1].reshape(flat),
        grads_back[:, :, 2].reshape(flat),
    )
    return (attn_out, query_grad, key_grad, value_grad, weight_grad)


def solution(mesh):
    placed = (
        P("dp", "seq", None),
        P("dp", "seq", None),
        P("dp", "seq", None),
        P("dp", "seq", None),
        P("seq", None, "dp"),
        P(),
        P(),
    )
    return jax.shard_map(
        on_device,
        mesh=mesh,
        in_specs=placed,
        out_specs=(
            P("dp", "seq", None),
            P("dp", "seq", None),
            P("dp", "seq", None),
            P("dp", "seq", None),
            P("seq", None, "dp"),
        ),
        check_vma=False,
    )
```

```python
import functools

import jax
import jax.numpy as jnp
from jax import lax
from jax.experimental import pallas as pl
from jax.experimental.pallas import tpu as pltpu
from jax.sharding import PartitionSpec as P

F32 = jnp.float32
BF16 = jnp.bfloat16
NT = (((1,), (1,)), ((), ()))
TN = (((0,), (0,)), ((), ()))
NN = (((1,), (0,)), ((), ()))


def dot(a, b, dims):
    return lax.dot_general(a, b, dims, preferred_element_type=F32)


def slot_numbers(head_owner, most):
    count = head_owner.shape[0]
    same = head_owner[:, None] == head_owner[None, :]
    earlier = jnp.arange(count)[None, :] < jnp.arange(count)[:, None]
    rank = jnp.sum(jnp.logical_and(same, earlier), axis=1).astype(jnp.int32)
    return head_owner * most + rank


def gather_kernel(
    scale, bias_ref, sent_ref, dy_ref, weight_ref, qkv_ref, dy_all, out_ref, lse_ref, grad_ref,
    weight_all, dy_block, own_sem, qkv_send, qkv_recv, weight_send, weight_recv,
    right_send, left_send, chain_recv, pair_send, pair_recv, load_sem,
):
    seq, most, _, rows, dim = qkv_ref.shape
    dps = weight_all.shape[0]
    chips = seq // 2
    me, dp = lax.axis_index("seq"), lax.axis_index("dp")
    chip, core = me // 2, lax.rem(me, 2)
    pair = me + 1 - 2 * core

    def remote(source, target, send_sem, recv_sem, where):
        return pltpu.make_async_remote_copy(
            src_ref=source, dst_ref=target, send_sem=send_sem, recv_sem=recv_sem,
            device_id=where, device_id_type=pl.DeviceIdType.MESH,
        )

    barrier = pltpu.get_barrier_semaphore()
    for k in range(1, seq):
        pl.semaphore_signal(
            barrier, inc=1, device_id=(dp, lax.rem(me + k, seq)), device_id_type=pl.DeviceIdType.MESH
        )
    for k in range(1, dps):
        pl.semaphore_signal(
            barrier, inc=1, device_id=(lax.rem(dp + k, dps), me), device_id_type=pl.DeviceIdType.MESH
        )
    pl.semaphore_wait(barrier, seq - 1 + dps - 1)

    own = [
        pltpu.make_async_copy(sent_ref.at[me], qkv_ref.at[me], own_sem.at[0]),
        pltpu.make_async_copy(dy_ref.at[0], dy_all.at[me], own_sem.at[1]),
        pltpu.make_async_copy(weight_ref, weight_all.at[dp], own_sem.at[2]),
    ]
    qkv_copies = []
    for k in range(1, seq):
        to = lax.rem(me + k, seq)
        qkv_copies.append(
            remote(sent_ref.at[to], qkv_ref.at[me], qkv_send.at[k], qkv_recv.at[k], (dp, to))
        )
    weight_copies = [
        remote(weight_ref, weight_all.at[dp], weight_send.at[k], weight_recv.at[k],
               (lax.rem(dp + k, dps), me))
        for k in range(1, dps)
    ]

    def right_copy(source, origin):
        return remote(source, dy_all.at[2 * origin + core], right_send.at[origin],
                      chain_recv.at[origin], (dp, me + 2))

    def left_copy(source, origin):
        return remote(source, dy_all.at[2 * origin + core], left_send.at[origin],
                      chain_recv.at[origin], (dp, me - 2))

    def pair_copy(source, origin):
        return remote(source, dy_all.at[2 * origin + core], pair_send.at[origin],
                      pair_recv.at[origin], (dp, pair))

    for copy in qkv_copies + weight_copies + own:
        copy.start()

    @pl.when(chip + 1 < chips)
    def _():
        right_copy(dy_ref.at[0], chip).start()

    @pl.when(chip > 0)
    def _():
        left_copy(dy_ref.at[0], chip).start()

    pair_copy(dy_ref.at[0], chip).start()

    def pass_on(step):
        @pl.when(chip - 1 - step >= 0)
        def _():
            origin = chip - 1 - step
            block = dy_all.at[2 * origin + core]
            right_copy(block, origin).wait_recv()

            @pl.when(chip + 1 < chips)
            def _():
                right_copy(block, origin).start()

            pair_copy(block, origin).start()

        @pl.when(chip + 1 + step < chips)
        def _():
            origin = chip + 1 + step
            block = dy_all.at[2 * origin + core]
            left_copy(block, origin).wait_recv()

            @pl.when(chip > 0)
            def _():
                left_copy(block, origin).start()

            pair_copy(block, origin).start()

    for copy in qkv_copies:
        copy.wait_recv()
    own[0].wait()

    def forward(slot):
        keys = qkv_ref[:, slot, 1].reshape(seq * rows, dim)
        values = qkv_ref[:, slot, 2].reshape(seq * rows, dim)

        @pl.loop(0, seq)
        def _(i):
            q = qkv_ref[i, slot, 0]
            scores = dot(keys, q, NT) * scale
            parts = [
                scores[j * rows : (j + 1) * rows] + bias_ref[slot, i, j] for j in range(seq)
            ]
            top = jnp.max(functools.reduce(jnp.maximum, parts), axis=0, keepdims=True)
            parts = [jnp.exp(part - top) for part in parts]
            total = jnp.sum(functools.reduce(jnp.add, parts), axis=0, keepdims=True)
            inverse = 1.0 / total
            low = jnp.concatenate([(part * inverse).astype(BF16) for part in parts], axis=0)
            out_ref[i, slot] = dot(low, values, TN).astype(BF16)
            lse_ref[slot, pl.ds(i, 1), :] = top + jnp.log(total)

    def project(block):
        load = pltpu.make_async_copy(dy_all.at[block], dy_block, load_sem)
        load.start()
        load.wait()
        part_width = weight_all.shape[3]
        total = None
        for d in range(dps):
            term = dot(
                dy_block[:, d * part_width : (d + 1) * part_width],
                weight_all[d].reshape(most * dim, part_width), NT,
            )
            total = term if total is None else total + term
        for s in range(most):
            grad_ref[s, pl.ds(pl.multiple_of(block * rows, rows), rows), :] = total[
                :, s * dim : (s + 1) * dim
            ].astype(BF16)

    def project_ring(k):
        for origin, wanted in (
            (chip - k, chip - k >= 0),
            (chip + k, jnp.logical_and(k > 0, chip + k < chips)),
        ):
            @pl.when(wanted)
            def _(origin=origin):
                project(2 * origin + core)
                pair_copy(dy_all.at[2 * origin + core], origin).wait_recv()
                project(2 * origin + 1 - core)

    for step in range(max(chips - 1, most)):
        if step < most:
            forward(step)
        if step < chips - 1:
            pass_on(step)
        if step == 0:
            own[1].wait()
            own[2].wait()
            for copy in weight_copies:
                copy.wait_recv()
        if step < chips - 1:
            project_ring(step)
    project_ring(chips - 1)

    for copy in qkv_copies + weight_copies:
        copy.wait_send()
    for origin in range(chips):
        block = dy_all.at[2 * origin + core]
        pair_copy(block, origin).wait_send()

        @pl.when(jnp.logical_and(chip + 1 < chips, origin <= chip))
        def _():
            right_copy(block, origin).wait_send()

        @pl.when(jnp.logical_and(chip > 0, origin >= chip))
        def _():
            left_copy(block, origin).wait_send()


def backward_kernel(
    scale, grad_scale, bias_ref, qkv_ref, out_ref, lse_ref, grad_ref, dy_ref,
    out_back, grads_back, weight_back,
    grads_ref, dk_ref, dv_ref, dy_part, weight_part,
    own_sem, own_grad_sem, out_send, out_recv, grads_send, grads_recv, weight_send, weight_recv, load_sem,
):
    seq, most, _, rows, dim = qkv_ref.shape
    dps, part_width = weight_part.shape[0], weight_part.shape[3]
    me, dp = lax.axis_index("seq"), lax.axis_index("dp")

    def remote(source, target, send_sem, recv_sem, where):
        return pltpu.make_async_remote_copy(
            src_ref=source, dst_ref=target, send_sem=send_sem, recv_sem=recv_sem,
            device_id=where, device_id_type=pl.DeviceIdType.MESH,
        )

    def load(k):
        column = pl.multiple_of(lax.rem(dp + k, dps) * part_width, 128)
        return pltpu.make_async_copy(
            dy_ref.at[:, :, pl.ds(column, part_width)], dy_part.at[k % 2], load_sem.at[k % 2]
        )

    load(1 % dps).start()
    barrier = pltpu.get_barrier_semaphore()
    for k in range(1, seq):
        pl.semaphore_signal(
            barrier, inc=1, device_id=(dp, lax.rem(me + k, seq)), device_id_type=pl.DeviceIdType.MESH
        )
    for k in range(1, dps):
        pl.semaphore_signal(
            barrier, inc=1, device_id=(lax.rem(dp + k, dps), me), device_id_type=pl.DeviceIdType.MESH
        )
    pl.semaphore_wait(barrier, seq - 1 + dps - 1)

    pending = []
    own = [pltpu.make_async_copy(out_ref.at[me], out_back.at[me], own_sem.at[0])]
    own[0].start()
    for k in range(1, seq):
        to = lax.rem(me + k, seq)
        copy = remote(out_ref.at[to], out_back.at[me], out_send.at[k], out_recv.at[k], (dp, to))
        copy.start()
        pending.append(copy)

    order = list(range(1, dps)) + [dps]
    for k in order:
        part = lax.rem(dp + k, dps)
        load(k).wait()
        if k < dps:
            load(k + 1).start()

        @pl.loop(0, most)
        def _(slot):
            rows_out = out_ref[:, slot].reshape(seq * rows, dim)
            total = dot(rows_out, dy_part[k % 2].reshape(seq * rows, part_width), TN)
            weight_part[part, slot] = (total * grad_scale).astype(BF16)

        if k < dps:
            copy = remote(weight_part.at[part], weight_back.at[dp], weight_send.at[k],
                          weight_recv.at[k], (part, me))
            pending.append(copy)
        else:
            copy = pltpu.make_async_copy(weight_part.at[dp], weight_back.at[dp], own_sem.at[1])
            own.append(copy)
        copy.start()

    for slot in range(most):
        keys = qkv_ref[:, slot, 1].reshape(seq * rows, dim)
        values = qkv_ref[:, slot, 2].reshape(seq * rows, dim)
        dk_ref[...] = jnp.zeros_like(dk_ref)
        dv_ref[...] = jnp.zeros_like(dv_ref)

        @pl.loop(0, seq)
        def _(i):
            q = qkv_ref[i, slot, 0]
            g = grad_ref[slot, pl.ds(pl.multiple_of(i * rows, rows), rows), :]
            product = g.astype(F32) * out_ref[i, slot].astype(F32)
            delta = jnp.sum(product.T, axis=0, keepdims=True)
            lse = lse_ref[slot, pl.ds(i, 1), :]
            scores = dot(keys, q, NT) * scale
            prob_grad = dot(values, g, NT)
            lows, score_grads = [], []
            for j in range(seq):
                part = slice(j * rows, (j + 1) * rows)
                prob = jnp.exp(scores[part] + (bias_ref[slot, i, j] - lse))
                lows.append(prob.astype(BF16))
                score_grads.append((prob * (prob_grad[part] - delta) * scale).astype(BF16))
            low = jnp.concatenate(lows, axis=0)
            score_grad = jnp.concatenate(score_grads, axis=0)
            dv_ref[...] += dot(low, g, NN)
            dk_ref[...] += dot(score_grad, q, NN)
            grads_ref[i, slot, 0] = dot(score_grad, keys, TN).astype(BF16)

        grads_ref[:, slot, 1] = dk_ref[...].astype(BF16).reshape(seq, rows, dim)
        grads_ref[:, slot, 2] = dv_ref[...].astype(BF16).reshape(seq, rows, dim)
        for k in range(1, seq):
            to = lax.rem(me + k, seq)
            copy = remote(grads_ref.at[to, slot], grads_back.at[me, slot], grads_send.at[slot, k],
                          grads_recv.at[slot, k], (dp, to))
            copy.start()
            pending.append(copy)
        copy = pltpu.make_async_copy(
            grads_ref.at[me, slot], grads_back.at[me, slot], own_grad_sem.at[slot]
        )
        copy.start()
        own.append(copy)

    for copy in own + pending:
        copy.wait()


def tokens_kernel(
    slot_ref, used_ref, out_ref, grads_ref, weight_ref, attn_out, query_grad, key_grad, value_grad,
    weight_grad,
):
    dim = out_ref.shape[-1]
    for h in range(slot_ref.shape[0]):
        columns = slice(h * dim, (h + 1) * dim)
        slot = slot_ref[h]
        attn_out[0, :, columns] = out_ref[slot]
        query_grad[0, :, columns] = grads_ref[slot, 0]
        key_grad[0, :, columns] = grads_ref[slot, 1]
        value_grad[0, :, columns] = grads_ref[slot, 2]
    for s in range(weight_grad.shape[0]):
        total = functools.reduce(
            jnp.add, [weight_ref[d, s].astype(F32) for d in range(weight_ref.shape[0])]
        )
        weight_grad[s] = jnp.where(used_ref[s] > 0, total, 0.0)


SMEM = pl.BlockSpec(memory_space=pltpu.SMEM)
VMEM = pl.BlockSpec(memory_space=pltpu.VMEM)
ANY = pl.BlockSpec(memory_space=pl.ANY)
PARAMS = pltpu.CompilerParams(vmem_limit_bytes=48 * 1024 * 1024)


def on_device(query_tok, key_tok, value_tok, grad_out, out_weight, block_mask, head_owner):
    seq = lax.axis_size("seq")
    dps = lax.axis_size("dp")
    most, dim, part_width = out_weight.shape
    rows = query_tok.shape[1]
    heads = block_mask.shape[0]
    tiles = block_mask.shape[1]
    length = seq * rows
    width = grad_out.shape[2]
    scale = dim ** (-0.5)
    grad_scale = (dps * length) ** (-0.5)
    slots = slot_numbers(head_owner, most)
    table = slots[:, None] == jnp.arange(seq * most, dtype=jnp.int32)[None, :]
    select = table.astype(BF16)
    mine = lax.dynamic_slice_in_dim(table, lax.axis_index("seq") * most, most, 1)
    used = jnp.any(mine, axis=0)
    kept = jnp.any(
        jnp.logical_and(mine[:, :, None, None], block_mask[:, None] > 0), axis=0
    ) | jnp.logical_not(used)[:, None, None]
    bias = jnp.where(kept, 0.0, -jnp.inf).astype(F32)

    def to_slots(tensor):
        split = tensor[0].reshape(rows, heads, dim)
        spread = jnp.einsum("thd,hj->jtd", split, select, preferred_element_type=F32)
        return spread.astype(BF16).reshape(seq, most, 1, rows, dim)

    sent = jnp.concatenate([to_slots(t) for t in (query_tok, key_tok, value_tok)], axis=2)
    chips = seq // 2
    dma = pltpu.SemaphoreType.DMA
    qkv, dy, slot_out, lse, grad_attn = pl.pallas_call(
        functools.partial(gather_kernel, scale),
        out_shape=(
            jax.ShapeDtypeStruct((seq, most, 3, rows, dim), BF16),
            jax.ShapeDtypeStruct((seq, rows, width), BF16),
            jax.ShapeDtypeStruct((seq, most, rows, dim), BF16),
            jax.ShapeDtypeStruct((most, tiles, rows), F32),
            jax.ShapeDtypeStruct((most, length, dim), BF16),
        ),
        in_specs=[SMEM, ANY, ANY, ANY],
        out_specs=(VMEM, ANY, VMEM, VMEM, VMEM),
        scratch_shapes=[
            pltpu.VMEM((dps, most, dim, part_width), BF16),
            pltpu.VMEM((rows, width), BF16),
            dma((3,)), dma((seq,)), dma((seq,)), dma((dps,)), dma((dps,)),
            dma((chips,)), dma((chips,)), dma((chips,)), dma((chips,)), dma((chips,)),
            dma(()),
        ],
        compiler_params=pltpu.CompilerParams(
            vmem_limit_bytes=48 * 1024 * 1024, collective_id=0, has_side_effects=True
        ),
        name="gather_forward",
    )(bias, sent, grad_out, out_weight)
    out_back, grads_back, weight_back = pl.pallas_call(
        functools.partial(backward_kernel, scale, grad_scale),
        out_shape=(
            jax.ShapeDtypeStruct((seq, most, rows, dim), BF16),
            jax.ShapeDtypeStruct((seq, most, 3, rows, dim), BF16),
            jax.ShapeDtypeStruct((dps, most, dim, part_width), BF16),
        ),
        in_specs=[SMEM, VMEM, VMEM, VMEM, VMEM, ANY],
        out_specs=(ANY,) * 3,
        scratch_shapes=[
            pltpu.VMEM((seq, most, 3, rows, dim), BF16),
            pltpu.VMEM((length, dim), F32),
            pltpu.VMEM((length, dim), F32),
            pltpu.VMEM((2, seq, rows, part_width), BF16),
            pltpu.VMEM((dps, most, dim, part_width), BF16),
            dma((2,)), dma((most,)), dma((seq,)), dma((seq,)), dma((most, seq)), dma((most, seq)),
            dma((dps,)), dma((dps,)), dma((2,)),
        ],
        compiler_params=pltpu.CompilerParams(
            vmem_limit_bytes=48 * 1024 * 1024, collective_id=1, has_side_effects=True
        ),
        name="backward_return",
    )(bias, qkv, slot_out, lse, grad_attn, dy)

    token_shape = jax.ShapeDtypeStruct((1, rows, heads * dim), BF16)
    attn_out, query_grad, key_grad, value_grad, weight_grad = pl.pallas_call(
        tokens_kernel,
        out_shape=(token_shape,) * 4 + (jax.ShapeDtypeStruct(out_weight.shape, F32),),
        in_specs=[SMEM, SMEM] + [VMEM] * 3,
        out_specs=(VMEM,) * 5,
        compiler_params=PARAMS,
        name="heads_to_tokens",
    )(
        slots,
        used.astype(jnp.int32),
        out_back.reshape(seq * most, rows, dim),
        grads_back.reshape(seq * most, 3, rows, dim),
        weight_back,
    )
    return (attn_out, query_grad, key_grad, value_grad, weight_grad)


def solution(mesh):
    placed = (
        P("dp", "seq", None),
        P("dp", "seq", None),
        P("dp", "seq", None),
        P("dp", "seq", None),
        P("seq", None, "dp"),
        P(),
        P(),
    )
    return jax.shard_map(
        on_device,
        mesh=mesh,
        in_specs=placed,
        out_specs=(
            P("dp", "seq", None),
            P("dp", "seq", None),
            P("dp", "seq", None),
            P("dp", "seq", None),
            P("seq", None, "dp"),
        ),
        check_vma=False,
    )
```
